32 devices in a mesh: wa: 16 (over z, y, x), row: 2 (over core).
Axes of the slice: x: 2, y: 2, z: 4, core: 2. Of those that a mesh axis runs over, the one named last changes fastest.
Arguments:
- tokens: bfloat16 [2048, 12288], P('wa', 'row'), may hold values from -6 to 6
- active: int32 [16, 48], replicated, may hold values from 0 to 383, all different within a row; in each aligned block of 16 rows (0 to 15, 16 to 31, ...) at most 2 rows name the same one
- w_up: bfloat16 [12288, 49152], P('row', 'wa'), may hold values from -0.0546875 to 0.0546875
- b_up: float32 [49152], P('wa'), may hold values from -3 to 3
- w_down: bfloat16 [49152, 12288], P('wa', 'row'), may hold values from -0.078125 to 0.078125
- b_down: float32 [12288], P('row'), may hold values from -3 to 3
Outputs:
- mixed: bfloat16 [2048, 12288], P('wa', 'row')
The draws below stay inside these ranges and needn't reach their ends.
Inputs may be any that keep to these rules, and one draw needn't show every extreme that they name: Row t lists 48 different neuron blocks active for token block t. Every neuron block is named by at least one and at most 2 token blocks, and one by exactly 2.
All inputs are finite; a program needn't handle non-finite values.
Results may differ from the reference program's by a relative error of at most 0.025.
Values may be sent and summed in bfloat16 or wider, within the bound.
No kernel may reach another device: no remote copies, remote signals or barrier semaphores. Data moves between devices by JAX's collectives and lax.ppermute only.
A program may use at most 320 MiB of HBM per device.

```python
import math
import jax
import jax.numpy as jnp
import numpy as np
from jax import lax

D = 12288
FF = 49152
BLK = 128
K = 48
TOKENS = 2048
TBLOCKS = 16
NB = 384
CAP = 2
N_WA = 16


def block_scale(own_key, extent, shards, least, top_value):
    def one(axis_at, shards_of):
        heights = jax.random.uniform(jax.random.fold_in(jax.random.fold_in(own_key, 6), axis_at), (shards_of,), jnp.float32, least / len(shards), top_value / len(shards))
        return jnp.repeat(jnp.exp(heights), extent[axis_at] // shards_of).reshape((-1,) + (1,) * (len(extent) - axis_at - 1))

    gain = one(*shards[0])
    for cut in shards[1:]:
        gain = gain * one(*cut)
    return gain


def assign_block(rng, own, number, rows, number_of, top, most, slope):
    sequence = jax.random.permutation(rng, number_of)
    crowded, common = shares(number_of, rows * top, most, slope, True), shares(number_of, rows * top, most, slope, False)
    places = jnp.arange(number_of)

    def named(sizes, turn):
        used = int((sizes > 0).sum())
        fixed = max(1, used // 4)
        shifted = fixed + (places - fixed + turn * (used - fixed)) % max(1, number_of - fixed)
        return jnp.zeros((number_of,), jnp.int32).at[sequence[jnp.where(places < fixed, places, shifted)]].set(jnp.asarray(sizes, jnp.int32))

    sizes = jnp.where(number % 4 == 0, named(crowded, number // 4), named(common, number - number // 4 - 1))
    mixed = jax.random.permutation(jax.random.fold_in(own, 3), number_of)
    giver, receiver = mixed[0:number_of // 2 * 2:2], mixed[1:number_of // 2 * 2:2]
    slack = jnp.minimum(sizes[giver] - 1, most - sizes[receiver]) // 2
    slack = jnp.where((giver == sequence[0]) | (receiver == sequence[0]) | (sizes[receiver] == 0), 0, jnp.maximum(slack, 0))
    shifted = jax.random.randint(jax.random.fold_in(own, 4), (number_of // 2,), 0, 1 << 20) % (slack + 1)
    sizes = sizes.at[giver].add(-shifted).at[receiver].add(shifted)
    members = jnp.searchsorted(jnp.cumsum(sizes), jnp.arange(rows * top), side="right").astype(jnp.int32)
    grid = members.reshape(top, rows).T
    grid = grid[jax.random.permutation(jax.random.fold_in(own, 1), rows)]
    turn = jax.random.randint(jax.random.fold_in(own, 2), (rows, 1), 0, top)
    return jnp.take_along_axis(grid, (jnp.arange(top)[None, :] + turn) % top, axis=1)


def shares(count, total, most, skew, full):
    portions = [(1 << 20) // math.isqrt(grade ** skew) + 1 for grade in range(1, count + 1)]
    largest = most if full else min(most, max(-(-total // count), total * portions[0] // sum(portions)))
    least = 1 if total - largest >= count - 1 else 0
    given, surplus = [largest] + [least] * (count - 1), total - largest - least * (count - 1)
    while surplus > 0:
        movable = [i for i in range(1, count) if given[i] < largest] or [i for i in range(1, count) if given[i] < most]
        pool, budget = sum([portions[i] for i in movable]), surplus
        for i in movable:
            addition = min(most - given[i], max(1, budget * portions[i] // pool), surplus)
            given[i] = given[i] + addition
            surplus = surplus - addition
    return np.array(given)


def normal_values(stream_key, shape, deviation, bound, pieces=(), kind=jnp.bfloat16):
    result = jax.random.normal(stream_key, shape, jnp.float32) * deviation
    if len(pieces) > 0:
        result = block_scale(stream_key, shape, pieces, -0.22, 0.18) * result
    return jnp.clip(result, min=-bound, max=bound).astype(kind)


def setup_inputs(seed: int = 0) -> dict:
    key_list = jax.random.split(jax.random.key(seed), 7)
    tokens = normal_values(key_list[0], (TOKENS, D), 1.0, 6.0, ((0, 16), (1, 2)))
    active_keys = jax.random.split(jax.random.fold_in(key_list[1], 1), TBLOCKS // TBLOCKS)
    active_turns = jax.random.permutation(jax.random.fold_in(key_list[1], 3), TBLOCKS // TBLOCKS)
    active = jax.vmap(lambda own, number: assign_block(jax.random.fold_in(key_list[1], 2), own, number, TBLOCKS, NB, K, CAP, 2))(active_keys, active_turns).reshape((TBLOCKS, K))
    w_up = normal_values(key_list[2], (D, FF), D ** -0.5, 0.0546875, ((0, 2), (1, 16)))
    b_up = normal_values(key_list[3], (FF,), 0.5, 3.0, ((0, 16),), jnp.float32)
    w_down = normal_values(key_list[4], (FF, D), (K * BLK) ** -0.5, 0.078125, ((0, 16), (1, 2)))
    b_down = normal_values(key_list[5], (D,), 0.5, 3.0, ((0, 2),), jnp.float32)
    return {"tokens": tokens, "active": active, "w_up": w_up, "b_up": b_up, "w_down": w_down, "b_down": b_down}


def reference(tokens, active, w_up, b_up, w_down, b_down):
    nblocks = FF // BLK
    per_owner = nblocks // N_WA
    up_blocks = w_up.reshape(D, nblocks, BLK)
    down_blocks = w_down.reshape(nblocks, BLK, D)
    bias_blocks = b_up.reshape(nblocks, BLK)
    token_blocks = tokens.reshape(TBLOCKS, BLK, D)
    owners_all = jnp.arange(N_WA, dtype=jnp.int32)

    def one_block(pair):
        block_rows, chosen = pair
        chosen = chosen.astype(jnp.int32)
        up_sel = jnp.take(up_blocks, chosen, axis=1).reshape(D, K * BLK)
        bias_sel = jnp.take(bias_blocks, chosen, axis=0).reshape(K * BLK)
        preact = jnp.dot(block_rows, up_sel, preferred_element_type=jnp.float32) + bias_sel
        hidden = jnp.maximum(preact, 0.0).astype(jnp.bfloat16)
        hidden = lax.optimization_barrier(hidden)
        hidden = hidden.astype(jnp.float32).reshape(BLK, K, BLK)
        down_sel = jnp.take(down_blocks, chosen, axis=0).astype(jnp.float32)
        contrib = jnp.einsum("qkb,kbd->kqd", hidden, down_sel)
        owner_of = chosen // per_owner
        onehot = (owner_of[:, None] == owners_all[None, :]).astype(jnp.float32)
        partial_value = jnp.einsum("kw,kqd->wqd", onehot, contrib, precision=lax.Precision.HIGHEST)
        partial_value = partial_value.astype(jnp.bfloat16)
        partial_value = lax.optimization_barrier(partial_value)
        total = jnp.sum(partial_value.astype(jnp.float32), axis=0) + b_down
        return total.astype(jnp.bfloat16)

    mixed = lax.map(one_block, (token_blocks, active))
    return mixed.reshape(TOKENS, D)
```

```python
import functools

import jax
import jax.numpy as jnp
from jax import lax
from jax.experimental import pallas as pl
from jax.experimental.pallas import tpu as pltpu
from jax.sharding import PartitionSpec as P

BLK = 128
K = 48
HALF = BLK // 2
PLANE = 4
LAYERS = 4
DEPTH = 3
VMEM_BYTES = 56 * 1024 * 1024


def stream(meta, per_owner, fetch, use):
    count = meta[0]

    def block(step):
        return lax.rem(meta[1 + step], per_owner)

    for ahead in range(DEPTH - 1):
        @pl.when(ahead < count)
        def _():
            fetch(block(ahead), ahead).start()

    def body(step, carry):
        nearest = step + DEPTH - 1

        @pl.when(nearest < count)
        def _():
            fetch(block(nearest), lax.rem(nearest, DEPTH)).start()

        slot = lax.rem(step, DEPTH)
        fetch(block(step), slot).wait()
        use(step, slot)
        return carry

    lax.fori_loop(0, count, body, 0)


def up_kernel(per_owner, meta, *refs):
    parts, (w_ref, own_ref, send_ref, rows, held, row_sems, sems) = refs[:2 * PLANE], refs[2 * PLANE:]
    copies = []
    for at, part in enumerate(parts):
        place = rows.at[at // 2, pl.ds((at % 2) * HALF, HALF)]
        copies.append(pltpu.make_async_copy(part, place, row_sems.at[at]))
    for copy in copies:
        copy.start()

    def fetch(block, slot):
        cols = pl.ds(pl.multiple_of(block * BLK, BLK), BLK)
        return pltpu.make_async_copy(w_ref.at[:, cols], held.at[slot], sems.at[slot])

    for copy in copies:
        copy.wait()

    def use(step, slot):
        offset = lax.div(meta[1 + step], per_owner)
        preact = jnp.dot(rows[offset], held[slot], preferred_element_type=jnp.float32)
        own_ref[step] = preact
        send_ref[step] = preact.astype(jnp.bfloat16)

    stream(meta, per_owner, fetch, use)


def estimate(feat):
    return pl.CostEstimate(flops=2 * 24 * BLK * BLK * feat, bytes_accessed=24 * BLK * feat * 2, transcendentals=0)


def up_group(meta, parts, w_up, slots):
    feat = w_up.shape[0]
    per_owner = w_up.shape[1] // BLK
    return pl.pallas_call(
        functools.partial(up_kernel, per_owner),
        in_specs=[pl.BlockSpec(memory_space=pltpu.SMEM)] + [pl.BlockSpec(memory_space=pl.ANY)] * (len(parts) + 1),
        out_specs=[pl.BlockSpec(memory_space=pltpu.VMEM)] * 2,
        scratch_shapes=[
            pltpu.VMEM((PLANE, BLK, feat), jnp.bfloat16),
            pltpu.VMEM((DEPTH, feat, BLK), jnp.bfloat16),
            pltpu.SemaphoreType.DMA((len(parts),)),
            pltpu.SemaphoreType.DMA((DEPTH,)),
        ],
        out_shape=[
            jax.ShapeDtypeStruct((slots, BLK, BLK), jnp.float32),
            jax.ShapeDtypeStruct((slots, BLK, BLK), jnp.bfloat16),
        ],
        compiler_params=pltpu.CompilerParams(vmem_limit_bytes=VMEM_BYTES),
        cost_estimate=estimate(feat),
        name="up_group",
    )(meta, *parts, w_up)


def down_kernel(per_owner, meta, own_ref, other_ref, bias_ref, w_ref, *refs):
    outs, (total, held, sems) = refs[:2 * PLANE], refs[2 * PLANE:]
    count = meta[0]
    width = total.shape[1]
    piece = width // 6 if width % (6 * BLK) == 0 else width
    for out in outs:
        out[...] = jnp.zeros_like(out)

    def fetch(block, slot):
        rows = pl.ds(pl.multiple_of(block * BLK, BLK), BLK)
        return pltpu.make_async_copy(w_ref.at[rows], held.at[slot], sems.at[slot])

    def use(step, slot):
        offset = lax.div(meta[1 + step], per_owner)
        block = lax.rem(meta[1 + step], per_owner)
        before = lax.div(meta[jnp.maximum(step, 1)], per_owner)
        after = lax.div(meta[2 + step], per_owner)
        first = (step == 0) | (before != offset)
        last = (step >= count - 1) | (after != offset)
        preact = own_ref[step] + other_ref[step].astype(jnp.float32) + bias_ref[block]
        hidden = jnp.maximum(preact, 0.0).astype(jnp.bfloat16)
        for at in range(0, width, piece):
            cols = pl.ds(at, piece)
            term = jnp.dot(hidden, held[slot, :, cols], preferred_element_type=jnp.float32)
            total[:, cols] = jnp.where(first, 0.0, total[:, cols]) + term

        for o in range(PLANE):
            @pl.when(last & (offset == o))
            def _():
                outs[2 * o][...] = total[:HALF].astype(jnp.bfloat16)
                outs[2 * o + 1][...] = total[HALF:].astype(jnp.bfloat16)

    stream(meta, per_owner, fetch, use)


def down_group(meta, own, other, bias, w_down):
    feat = w_down.shape[1]
    per_owner = w_down.shape[0] // BLK
    whole = pl.BlockSpec(memory_space=pltpu.VMEM)
    outs = pl.pallas_call(
        functools.partial(down_kernel, per_owner),
        in_specs=[pl.BlockSpec(memory_space=pltpu.SMEM), whole, whole, whole, pl.BlockSpec(memory_space=pl.ANY)],
        out_specs=[whole] * (2 * PLANE),
        scratch_shapes=[
            pltpu.VMEM((BLK, feat), jnp.float32),
            pltpu.VMEM((DEPTH, BLK, feat), jnp.bfloat16),
            pltpu.SemaphoreType.DMA((DEPTH,)),
        ],
        out_shape=[jax.ShapeDtypeStruct((HALF, feat), jnp.bfloat16)] * (2 * PLANE),
        compiler_params=pltpu.CompilerParams(vmem_limit_bytes=VMEM_BYTES),
        cost_estimate=estimate(feat),
        name="down_group",
    )(meta, own, other, bias, w_down)
    return [(outs[2 * o], outs[2 * o + 1]) for o in range(PLANE)]


def in_plane(value, bit):
    owners = LAYERS * PLANE
    return lax.ppermute(value, "wa", [(w, w ^ bit) for w in range(owners)])


def along_z(value, *hops):
    pairs = [(a * PLANE + q, b * PLANE + q) for a, b in hops for q in range(PLANE)]
    return lax.ppermute(value, "wa", pairs)


def gather_plane(block):
    a0, b0 = block
    a1, b2 = in_plane(a0, 1), in_plane(b0, 2)
    a2, a3 = in_plane(a0, 2), in_plane(a1, 2)
    b1, b3 = in_plane(b0, 1), in_plane(b2, 1)
    return [a0, b0, a1, b1, a2, b2, a3, b3]


def add(*terms):
    total = terms[0].astype(jnp.float32)
    for term in terms[1:]:
        total = total + term.astype(jnp.float32)
    return total


def narrow(*terms):
    return add(*terms).astype(jnp.bfloat16)


def reduce_plane(partial):
    (a0, b0), (a1, b1), (a2, b2), (a3, b3) = partial
    from_a2, from_a3 = in_plane(a2, 2), in_plane(a3, 2)
    from_b1, from_b3 = in_plane(b1, 1), in_plane(b3, 1)
    from_a1 = in_plane(narrow(a1, from_a3), 1)
    from_b2 = in_plane(narrow(b2, from_b3), 2)
    return add(a0, from_a2, from_a1), add(b0, from_b1, from_b2)


def join(halves):
    return jnp.concatenate(halves, axis=0)


def pair_lists(active, owner, per_owner):
    layer, cell = owner // PLANE, owner % PLANE
    order = jnp.array([[0, 1, 2, 3], [1, 2, 3, 0], [2, 1, 0, 3], [3, 2, 1, 0]], jnp.int32)
    layers = jnp.sum(jnp.where(jnp.arange(LAYERS)[:, None] == layer, order, 0), axis=0)
    blocks = layers[:, None] * PLANE + (cell ^ jnp.arange(PLANE, dtype=jnp.int32))[None, :]
    targets = owner * per_owner + jnp.arange(per_owner, dtype=jnp.int32)
    hits = jnp.any(active[:, :, None] == targets[None, None, :], axis=1)
    is_block = blocks[:, :, None] == jnp.arange(active.shape[0], dtype=jnp.int32)
    hits = jnp.any(is_block[..., None] & hits[None, None], axis=2)
    hits = hits.reshape(LAYERS, PLANE * per_owner).astype(jnp.int32)
    slots = 2 * per_owner
    number = jnp.cumsum(hits, axis=1) * hits
    codes = jnp.arange(PLANE * per_owner, dtype=jnp.int32)
    wanted = jnp.arange(slots + 8, dtype=jnp.int32) + 1
    lists = jnp.sum(jnp.where(number[:, :, None] == wanted, codes[None, :, None], 0), axis=1)
    counts = jnp.sum(hits, axis=1, keepdims=True)
    return jnp.concatenate([counts, lists], axis=1), slots


def by_layers(tokens, active, w_up, b_up, w_down, b_down):
    per_owner = w_up.shape[1] // BLK
    owner = lax.axis_index("wa")
    layer = owner // PLANE
    inner = (layer == 1) | (layer == 2)
    meta, slots = pair_lists(active, owner, per_owner)
    bias = b_up.reshape(per_owner, 1, BLK)

    inward = along_z(tokens, (0, 1), (3, 2))
    across = along_z(tokens, (1, 2), (2, 1))
    outward = along_z(tokens, (1, 0), (2, 3))
    across2 = along_z(inward, (1, 2), (2, 1))
    outward2 = along_z(across, (1, 0), (2, 3))
    outward3 = along_z(across2, (1, 0), (2, 3))

    def halves(inside, outside):
        return [jnp.where(inner, inside[rows], outside[rows]) for rows in (slice(0, HALF), slice(HALF, BLK))]

    groups = [
        [tokens[:HALF], tokens[HALF:]],
        halves(across, outward),
        halves(across2, outward2),
        halves(inward, outward3),
    ]
    partial = []
    for at, group in enumerate(groups):
        parts = gather_plane(group)
        own, send = up_group(meta[at], parts, w_up, slots)
        other = lax.ppermute(send, "row", [(0, 1), (1, 0)])
        partial.append(down_group(meta[at], own, other, bias, w_down))

    sums = {at: join(reduce_plane(partial[at])) for at in (2, 3, 1, 0)}
    from_corner = along_z(sums[3].astype(jnp.bfloat16), (0, 1), (3, 2))
    second = narrow(sums[2], from_corner)
    third = narrow(sums[3], along_z(second, (1, 2), (2, 1)))
    first = narrow(sums[1], along_z(second, (0, 1), (3, 2)))
    last = [
        along_z(third, (1, 0), (2, 3)),
        along_z(first, (1, 2), (2, 1)),
        along_z(first, (0, 1), (3, 2)),
    ]
    return (add(sums[0], *last) + b_down).astype(jnp.bfloat16)


def general(tokens, active, w_up, b_up, w_down, b_down):
    feat_dev = tokens.shape[1]
    tblocks = active.shape[0]
    owners = lax.axis_size("wa")
    per_owner = w_up.shape[1] // BLK
    nblocks = per_owner * owners
    capacity = max(2, 5 * tblocks * K // (4 * nblocks))
    gathered = lax.all_gather(tokens, "wa", axis=0, tiled=True)
    token_blocks = gathered.reshape(tblocks, BLK, feat_dev)
    owner = lax.axis_index("wa")
    targets = owner * per_owner + jnp.arange(per_owner, dtype=jnp.int32)
    hits = jnp.any(active[:, :, None] == targets[None, None, :], axis=1).astype(jnp.int32)
    running = jnp.cumsum(hits, axis=0)
    slots = jnp.arange(capacity, dtype=jnp.int32) + 1
    picked = hits[:, :, None] * (running[:, :, None] == slots[None, None, :]).astype(jnp.int32)
    block_index = jnp.arange(tblocks, dtype=jnp.int32)
    slot_tok = jnp.sum(picked * block_index[:, None, None], axis=0)
    selected = token_blocks[slot_tok.reshape(-1)].reshape(per_owner, capacity * BLK, feat_dev)
    up_local = w_up.reshape(feat_dev, per_owner, BLK)
    preact = jnp.einsum("jmd,djb->jmb", selected, up_local, preferred_element_type=jnp.float32)
    bias_local = b_up.reshape(per_owner, 1, BLK)
    summed = lax.psum(preact.astype(jnp.bfloat16), "row").astype(jnp.float32)
    hidden = jnp.maximum(summed + bias_local, 0.0).astype(jnp.bfloat16)
    down_local = w_down.reshape(per_owner, BLK, feat_dev)
    contrib = jnp.einsum("jmb,jbd->jmd", hidden, down_local, preferred_element_type=jnp.float32)
    contrib = contrib.reshape(per_owner, capacity, BLK, feat_dev)
    placing = picked.transpose(1, 2, 0).astype(jnp.float32)
    partial_value = jnp.einsum("jct,jcqd->tqd", placing, contrib, precision=lax.Precision.HIGHEST)
    terms = partial_value.reshape(tblocks * BLK, feat_dev).astype(jnp.bfloat16)
    total = lax.psum_scatter(terms, "wa", scatter_dimension=0, tiled=True).astype(jnp.float32)
    return (total + b_down).astype(jnp.bfloat16)


def solution(mesh):
    sizes = (mesh.shape["wa"], mesh.shape["row"])
    per_device = by_layers if sizes == (LAYERS * PLANE, 2) else general
    in_specs = (P("wa", "row"), P(), P("row", "wa"), P("wa"), P("wa", "row"), P("row"))
    out_specs = P("wa", "row")
    return jax.shard_map(
        per_device, mesh=mesh, in_specs=in_specs, out_specs=out_specs, check_vma=False
    )
```

```python
import functools

import jax
import jax.numpy as jnp
from jax import lax
from jax.experimental import pallas as pl
from jax.experimental.pallas import tpu as pltpu
from jax.sharding import PartitionSpec as P

BLK = 128
K = 48
HALF = BLK // 2
PLANE = 4
LAYERS = 4
DEPTH = 3
VMEM_BYTES = 56 * 1024 * 1024


def stream(meta, count, copies_of, ready, use):
    def each(step, slot, act):
        for copy, wanted in copies_of(step, slot):
            if wanted is None:
                act(copy)
            else:
                pl.when(wanted)(functools.partial(act, copy))

    def start(step, slot):
        each(step, slot, lambda copy: copy.start())

    for ahead in range(DEPTH - 1):
        @pl.when(ahead < count)
        def _():
            start(ahead, ahead)

    ready()

    def body(step, carry):
        nearest = step + DEPTH - 1

        @pl.when(nearest < count)
        def _():
            start(nearest, lax.rem(nearest, DEPTH))

        slot = lax.rem(step, DEPTH)
        each(step, slot, lambda copy: copy.wait())
        use(step, slot)
        return carry

    lax.fori_loop(0, count, body, 0)


def up_kernel(per_owner, meta, *refs):
    parts, refs = refs[:PLANE + 1], refs[PLANE + 1:]
    w_ref, own_ref, send_ref, rows, held, own, send, row_sems, sems, own_sems, send_sems = refs
    count = meta[0]
    places = [rows.at[0], rows.at[1], rows.at[2], rows.at[3, pl.ds(0, HALF)], rows.at[3, pl.ds(HALF, HALF)]]
    copies = [pltpu.make_async_copy(*ends, row_sems.at[at]) for at, ends in enumerate(zip(parts, places))]
    for copy in copies:
        copy.start()

    def ready():
        for copy in copies:
            copy.wait()

    def copies_of(step, slot):
        for side in range(2):
            code = meta[1 + 2 * step + side]
            block = lax.rem(jnp.maximum(code, 0), per_owner)
            cols = pl.ds(pl.multiple_of(block * BLK, BLK), BLK)
            place = held.at[slot, :, pl.ds(side * BLK, BLK)]
            yield pltpu.make_async_copy(w_ref.at[:, cols], place, sems.at[slot, side]), code >= 0 if side else None

    def results(step):
        slot = lax.rem(step, 2)
        pair = pl.ds(2 * step, 2)
        return (pltpu.make_async_copy(own.at[slot], own_ref.at[pair], own_sems.at[slot]),
                pltpu.make_async_copy(send.at[slot], send_ref.at[pair], send_sems.at[slot]))

    def use(step, slot):
        offset = lax.div(meta[1 + 2 * step], per_owner)
        preact = jnp.dot(rows[offset], held[slot], preferred_element_type=jnp.float32)

        @pl.when(step >= 2)
        def _():
            for copy in results(step - 2):
                copy.wait()

        at = lax.rem(step, 2)
        for side in range(2):
            cols = slice(side * BLK, (side + 1) * BLK)
            own[at, side] = preact[:, cols]
            send[at, side] = preact[:, cols].astype(jnp.bfloat16)
        for copy in results(step):
            copy.start()

    stream(meta, count, copies_of, ready, use)
    for back in (2, 1):
        @pl.when(count >= back)
        def _():
            for copy in results(count - back):
                copy.wait()


def estimate(feat):
    return pl.CostEstimate(flops=2 * BLK * BLK * feat, bytes_accessed=BLK * feat * 2, transcendentals=0)


def up_group(meta, parts, w_up, slots):
    feat = w_up.shape[0]
    per_owner = w_up.shape[1] // BLK
    anywhere = pl.BlockSpec(memory_space=pl.ANY)
    return pl.pallas_call(
        functools.partial(up_kernel, per_owner),
        in_specs=[pl.BlockSpec(memory_space=pltpu.SMEM)] + [anywhere] * (len(parts) + 1),
        out_specs=[anywhere] * 2,
        scratch_shapes=[
            pltpu.VMEM((PLANE, BLK, feat), jnp.bfloat16),
            pltpu.VMEM((DEPTH, feat, 2 * BLK), jnp.bfloat16),
            pltpu.VMEM((2, 2, BLK, BLK), jnp.float32),
            pltpu.VMEM((2, 2, BLK, BLK), jnp.bfloat16),
            pltpu.SemaphoreType.DMA((len(parts),)),
            pltpu.SemaphoreType.DMA((DEPTH, 2)),
            pltpu.SemaphoreType.DMA((2,)),
            pltpu.SemaphoreType.DMA((2,)),
        ],
        out_shape=[
            jax.ShapeDtypeStruct((slots, BLK, BLK), jnp.float32),
            jax.ShapeDtypeStruct((slots, BLK, BLK), jnp.bfloat16),
        ],
        compiler_params=pltpu.CompilerParams(vmem_limit_bytes=VMEM_BYTES),
        cost_estimate=estimate(feat),
        name="up_group",
    )(meta, *parts, w_up)


def down_kernel(per_owner, slots, meta, own_ref, other_ref, bias_ref, w_ref, *refs):
    outs, (total, held, own, other, done, sems, done_sems) = refs[:PLANE + 1], refs[PLANE + 1:]
    count = meta[0]
    width = total.shape[1]
    piece = width // 6 if width % (6 * BLK) == 0 else width

    def results(o):
        if o < PLANE - 1:
            return [pltpu.make_async_copy(done.at[o], outs[o], done_sems.at[o])]
        halves = [pl.ds(0, HALF), pl.ds(HALF, HALF)]
        return [pltpu.make_async_copy(done.at[o, half], outs[o + at], done_sems.at[o + at]) for at, half in enumerate(halves)]

    def copies_of(step, slot):
        pair = pl.ds(2 * step, 2)
        yield pltpu.make_async_copy(own_ref.at[pair], own.at[slot], sems.at[slot, 2]), None
        yield pltpu.make_async_copy(other_ref.at[pair], other.at[slot], sems.at[slot, 3]), None
        left, right = meta[1 + 2 * step], meta[2 + 2 * step]
        for side, code in enumerate((left, jnp.where(right < 0, left, right))):
            rows = pl.ds(pl.multiple_of(lax.rem(code, per_owner) * BLK, BLK), BLK)
            place = held.at[slot, pl.ds(side * BLK, BLK)]
            yield pltpu.make_async_copy(w_ref.at[rows], place, sems.at[slot, side]), None

    def hidden_of(slot, side, code):
        preact = own[slot, side] + other[slot, side].astype(jnp.float32) + bias_ref[lax.rem(code, per_owner)]
        return jnp.maximum(preact, 0.0)

    def use(step, slot):
        left, right = meta[1 + 2 * step], meta[2 + 2 * step]
        offset = lax.div(left, per_owner)
        before = lax.div(meta[jnp.maximum(2 * step - 1, 1)], per_owner)
        after = lax.div(meta[3 + 2 * step], per_owner)
        first = (step == 0) | (before != offset)
        last = (step >= count - 1) | (after != offset)
        one = hidden_of(slot, 0, left)
        two = jnp.where(right < 0, 0.0, hidden_of(slot, 1, jnp.maximum(right, 0)))
        hidden = jnp.concatenate([one, two], axis=1).astype(jnp.bfloat16)
        for at in range(0, width, piece):
            cols = pl.ds(at, piece)
            term = jnp.dot(hidden, held[slot, :, cols], preferred_element_type=jnp.float32)
            total[:, cols] = jnp.where(first, 0.0, total[:, cols]) + term

        @pl.when(last)
        def _():
            done[offset] = total[...].astype(jnp.bfloat16)

        for o in range(PLANE):
            @pl.when(last & (offset == o))
            def _():
                for copy in results(o):
                    copy.start()

    stream(meta, count, copies_of, lambda: None, use)
    for o in range(PLANE):
        @pl.when(meta[1 + slots + 2 + o] == 0)
        def _():
            done[o] = jnp.zeros_like(done[o])
            for copy in results(o):
                copy.start()

    for o in range(PLANE):
        for copy in results(o):
            copy.wait()


def down_group(meta, own, other, bias, w_down):
    feat = w_down.shape[1]
    per_owner = w_down.shape[0] // BLK
    anywhere = pl.BlockSpec(memory_space=pl.ANY)
    whole = pl.BlockSpec(memory_space=pltpu.VMEM)
    return pl.pallas_call(
        functools.partial(down_kernel, per_owner, own.shape[0]),
        in_specs=[pl.BlockSpec(memory_space=pltpu.SMEM), anywhere, anywhere, whole, anywhere],
        out_specs=[anywhere] * (PLANE + 1),
        scratch_shapes=[
            pltpu.VMEM((BLK, feat), jnp.float32),
            pltpu.VMEM((DEPTH, 2 * BLK, feat), jnp.bfloat16),
            pltpu.VMEM((DEPTH, 2, BLK, BLK), jnp.float32),
            pltpu.VMEM((DEPTH, 2, BLK, BLK), jnp.bfloat16),
            pltpu.VMEM((PLANE, BLK, feat), jnp.bfloat16),
            pltpu.SemaphoreType.DMA((DEPTH, 4)),
            pltpu.SemaphoreType.DMA((PLANE + 1,)),
        ],
        out_shape=[jax.ShapeDtypeStruct((rows, feat), jnp.bfloat16) for rows in (BLK, BLK, BLK, HALF, HALF)],
        compiler_params=pltpu.CompilerParams(vmem_limit_bytes=VMEM_BYTES),
        cost_estimate=estimate(feat),
        name="down_group",
    )(meta, own, other, bias, w_down)


def add_kernel(x_ref, y_ref, x_add, y_add, x_out, y_out):
    x_out[...] = (x_ref[...].astype(jnp.float32) + x_add[...].astype(jnp.float32)).astype(jnp.bfloat16)
    y_out[...] = (y_ref[...].astype(jnp.float32) + y_add[...].astype(jnp.float32)).astype(jnp.bfloat16)


def add_diagonal(over_x, over_y, x_add, y_add):
    feat = over_x.shape[1]
    steps = 3
    upper = pl.BlockSpec((HALF, feat // steps), lambda i: (0, i))
    lower = pl.BlockSpec((HALF, feat // steps), lambda i: (1, i))
    return pl.pallas_call(
        add_kernel,
        grid=(steps,),
        in_specs=[upper, lower, upper, upper],
        out_specs=[upper, lower],
        out_shape=[jax.ShapeDtypeStruct(over_x.shape, jnp.bfloat16)] * 2,
        input_output_aliases={0: 0, 1: 1},
        name="add_diagonal",
    )(over_x, over_y, x_add, y_add)


def swap(value, bits):
    return lax.ppermute(value, "wa", [(w, w ^ bits) for w in range(LAYERS * PLANE)])


def add(*terms):
    total = terms[0].astype(jnp.float32)
    for term in terms[1:]:
        total = total + term.astype(jnp.float32)
    return total


def narrow(*terms):
    return add(*terms).astype(jnp.bfloat16)


def pair_lists(active, owner, per_owner):
    layer, cell = owner // PLANE, owner % PLANE
    order = jnp.array([[0, 1, 2, 3], [1, 0, 2, 3], [2, 3, 1, 0], [3, 2, 1, 0]], jnp.int32)
    layers = jnp.sum(jnp.where(jnp.arange(LAYERS)[:, None] == layer, order, 0), axis=0)
    blocks = layers[:, None] * PLANE + (cell ^ jnp.arange(PLANE, dtype=jnp.int32))[None, :]
    targets = owner * per_owner + jnp.arange(per_owner, dtype=jnp.int32)
    hits = jnp.any(active[:, :, None] == targets[None, None, :], axis=1)
    is_block = blocks[:, :, None] == jnp.arange(active.shape[0], dtype=jnp.int32)
    hits = jnp.any(is_block[..., None] & hits[None, None], axis=2).astype(jnp.int32)
    counts = jnp.sum(hits, axis=2)
    padded = counts + counts % 2
    starts = jnp.cumsum(padded, axis=1) - padded
    number = (starts[:, :, None] + jnp.cumsum(hits, axis=2)) * hits
    number = number.reshape(LAYERS, PLANE * per_owner)
    slots = 2 * per_owner + PLANE
    codes = jnp.arange(PLANE * per_owner, dtype=jnp.int32) + 1
    wanted = jnp.arange(slots, dtype=jnp.int32) + 1
    lists = jnp.sum(jnp.where(number[:, :, None] == wanted, codes[None, :, None], 0), axis=1) - 1
    steps = jnp.sum(padded, axis=1, keepdims=True) // 2
    return jnp.concatenate([steps, lists, jnp.full((LAYERS, 2), -1, jnp.int32), counts], axis=1), slots


def along_z(value, *hops):
    pairs = [(a * PLANE + q, b * PLANE + q) for a, b in hops for q in range(PLANE)]
    return lax.ppermute(value, "wa", pairs)


def together(*values):
    return lax.optimization_barrier(values)


def sides(block):
    return swap(block, 1), swap(block, 2)


def sides2(blocks):
    return swap(blocks[0], 1), swap(blocks[1], 2)


def corner(over_x, over_y):
    return swap(over_x[:HALF], 2), swap(over_y[HALF:], 1)


def by_layers(tokens, active, w_up, b_up, w_down, b_down):
    per_owner = w_up.shape[1] // BLK
    owner = lax.axis_index("wa")
    inner = (owner // PLANE == 1) | (owner // PLANE == 2)
    meta, slots = pair_lists(active, owner, per_owner)
    bias = b_up.reshape(per_owner, 1, BLK)

    def up(at, block, side, diagonal):
        return up_group(meta[at], [block, *side, *diagonal], w_up, slots)

    def down(at, sums):
        other = lax.ppermute(sums[1], "row", [(0, 1), (1, 0)])
        return down_group(meta[at], sums[0], other, bias, w_down)

    def cross(partial):
        return swap(partial[3], 2), swap(partial[4], 1)

    def summed(partial, crossed):
        return add_diagonal(partial[1], partial[2], *crossed)

    near, middle, side0 = swap(tokens, PLANE), along_z(tokens, (1, 2), (2, 1)), sides(tokens)
    near, middle, side0 = together(near, middle, side0)
    diag0, side1 = corner(*side0), sides(near)
    across, outward = along_z(near, (1, 2), (2, 1)), along_z(middle, (1, 0), (2, 3))
    across, outward, side1, diag0 = together(across, outward, side1, diag0)
    far = jnp.where(inner, middle, outward)
    diag1, side2, outward = corner(*side1), sides(far), along_z(across, (1, 0), (2, 3))
    up0 = up(0, tokens, side0, diag0)
    outward, side2, diag1, up0 = together(outward, side2, diag1, up0)
    last = jnp.where(inner, across, outward)
    diag2, side3 = corner(*side2), sides(last)
    part0, up1 = down(0, up0), up(1, near, side1, diag1)
    side3, diag2, part0, up1 = together(side3, diag2, part0, up1)
    diag3, cross0 = corner(*side3), cross(part0)
    part1, up2 = down(1, up1), up(2, far, side2, diag2)
    up3 = up(3, last, side3, diag3)
    cross0, part1, up2, up3 = together(cross0, part1, up2, up3)
    cross1, part2, part3 = cross(part1), down(2, up2), down(3, up3)
    cross1, part2, part3 = together(cross1, part2, part3)
    cross3, cross2 = cross(part3), cross(part2)
    sent3 = summed(part3, cross3)
    sent3, cross2, part1, cross1, part0, cross0 = together(sent3, cross2, part1, cross1, part0, cross0)
    got3 = sides2(sent3)
    sent2 = summed(part2, cross2)
    got2 = sides2(sent2)
    sum3 = narrow(part3[0], *got3)
    passed = along_z(sum3, (0, 1), (3, 2))
    sent1, sent0 = summed(part1, cross1), summed(part0, cross0)
    got2, sum3, sent1, sent0 = together(got2, sum3, sent1, sent0)
    got1, got0 = sides2(sent1), sides2(sent0)
    sum2 = narrow(part2[0], *got2)
    passed = along_z(narrow(sum3, passed), (1, 2), (2, 1))
    inward = along_z(sum2, (0, 1), (3, 2))
    near = swap(narrow(part1[0], passed, *got1), PLANE)
    middle = along_z(narrow(sum2, inward), (1, 2), (2, 1))
    return (add(part0[0], *got0, near, middle) + b_down).astype(jnp.bfloat16)


def general(tokens, active, w_up, b_up, w_down, b_down):
    feat_dev = tokens.shape[1]
    tblocks = active.shape[0]
    owners = lax.axis_size("wa")
    per_owner = w_up.shape[1] // BLK
    nblocks = per_owner * owners
    capacity = max(2, 5 * tblocks * K // (4 * nblocks))
    gathered = lax.all_gather(tokens, "wa", axis=0, tiled=True)
    token_blocks = gathered.reshape(tblocks, BLK, feat_dev)
    owner = lax.axis_index("wa")
    targets = owner * per_owner + jnp.arange(per_owner, dtype=jnp.int32)
    hits = jnp.any(active[:, :, None] == targets[None, None, :], axis=1).astype(jnp.int32)
    running = jnp.cumsum(hits, axis=0)
    slots = jnp.arange(capacity, dtype=jnp.int32) + 1
    picked = hits[:, :, None] * (running[:, :, None] == slots[None, None, :]).astype(jnp.int32)
    block_index = jnp.arange(tblocks, dtype=jnp.int32)
    slot_tok = jnp.sum(picked * block_index[:, None, None], axis=0)
    selected = token_blocks[slot_tok.reshape(-1)].reshape(per_owner, capacity * BLK, feat_dev)
    up_local = w_up.reshape(feat_dev, per_owner, BLK)
    preact = jnp.einsum("jmd,djb->jmb", selected, up_local, preferred_element_type=jnp.float32)
    bias_local = b_up.reshape(per_owner, 1, BLK)
    summed = lax.psum(preact.astype(jnp.bfloat16), "row").astype(jnp.float32)
    hidden = jnp.maximum(summed + bias_local, 0.0).astype(jnp.bfloat16)
    down_local = w_down.reshape(per_owner, BLK, feat_dev)
    contrib = jnp.einsum("jmb,jbd->jmd", hidden, down_local, preferred_element_type=jnp.float32)
    contrib = contrib.reshape(per_owner, capacity, BLK, feat_dev)
    placing = picked.transpose(1, 2, 0).astype(jnp.float32)
    partial_value = jnp.einsum("jct,jcqd->tqd", placing, contrib, precision=lax.Precision.HIGHEST)
    terms = partial_value.reshape(tblocks * BLK, feat_dev).astype(jnp.bfloat16)
    total = lax.psum_scatter(terms, "wa", scatter_dimension=0, tiled=True).astype(jnp.float32)
    return (total + b_down).astype(jnp.bfloat16)


def solution(mesh):
    sizes = (mesh.shape["wa"], mesh.shape["row"])
    per_device = by_layers if sizes == (LAYERS * PLANE, 2) else general
    in_specs = (P("wa", "row"), P(), P("row", "wa"), P("wa"), P("wa", "row"), P("row"))
    out_specs = P("wa", "row")
    return jax.shard_map(
        per_device, mesh=mesh, in_specs=in_specs, out_specs=out_specs, check_vma=False
    )
```

```python
import functools

import jax
import jax.numpy as jnp
from jax import lax
from jax.experimental import pallas as pl
from jax.experimental.pallas import tpu as pltpu
from jax.sharding import PartitionSpec as P

BLK = 128
K = 48
HALF = BLK // 2
PLANE = 4
LAYERS = 4
DEPTH = 5
VMEM_BYTES = 56 * 1024 * 1024


def stream(meta, count, copies_of, ready, use):
    def each(step, slot, act):
        for copy, wanted in copies_of(step, slot):
            if wanted is None:
                act(copy)
            else:
                pl.when(wanted)(functools.partial(act, copy))

    def start(step, slot):
        each(step, slot, lambda copy: copy.start())

    for ahead in range(DEPTH - 1):
        @pl.when(ahead < count)
        def _():
            start(ahead, ahead)

    ready()

    def body(step, carry):
        nearest = step + DEPTH - 1

        @pl.when(nearest < count)
        def _():
            start(nearest, lax.rem(nearest, DEPTH))

        slot = lax.rem(step, DEPTH)
        each(step, slot, lambda copy: copy.wait())
        use(step, slot)
        return carry

    lax.fori_loop(0, count, body, 0)


def up_kernel(per_owner, meta, *refs):
    parts, refs = refs[:PLANE + 1], refs[PLANE + 1:]
    w_ref, own_ref, send_ref, rows, held, own, send, row_sems, sems, own_sems, send_sems = refs
    count = meta[0]
    places = [rows.at[0], rows.at[1], rows.at[2], rows.at[3, pl.ds(0, HALF)], rows.at[3, pl.ds(HALF, HALF)]]
    copies = [pltpu.make_async_copy(*ends, row_sems.at[at]) for at, ends in enumerate(zip(parts, places))]
    for copy in copies:
        copy.start()

    def ready():
        for copy in copies:
            copy.wait()

    def copies_of(step, slot):
        for side in range(2):
            code = meta[1 + 2 * step + side]
            block = lax.rem(jnp.maximum(code, 0), per_owner)
            cols = pl.ds(pl.multiple_of(block * BLK, BLK), BLK)
            place = held.at[slot, :, pl.ds(side * BLK, BLK)]
            yield pltpu.make_async_copy(w_ref.at[:, cols], place, sems.at[slot, side]), code >= 0 if side else None

    def results(step):
        slot = lax.rem(step, 2)
        pair = pl.ds(2 * step, 2)
        return (pltpu.make_async_copy(own.at[slot], own_ref.at[pair], own_sems.at[slot]),
                pltpu.make_async_copy(send.at[slot], send_ref.at[pair], send_sems.at[slot]))

    def use(step, slot):
        offset = lax.div(meta[1 + 2 * step], per_owner)
        preact = jnp.dot(rows[offset], held[slot], preferred_element_type=jnp.float32)

        @pl.when(step >= 2)
        def _():
            for copy in results(step - 2):
                copy.wait()

        at = lax.rem(step, 2)
        for side in range(2):
            cols = slice(side * BLK, (side + 1) * BLK)
            own[at, side] = preact[:, cols]
            send[at, side] = preact[:, cols].astype(jnp.bfloat16)
        for copy in results(step):
            copy.start()

    stream(meta, count, copies_of, ready, use)
    for back in (2, 1):
        @pl.when(count >= back)
        def _():
            for copy in results(count - back):
                copy.wait()


def estimate(feat):
    return pl.CostEstimate(flops=2 * BLK * BLK * feat, bytes_accessed=BLK * feat * 2, transcendentals=0)


def up_group(meta, parts, w_up, slots):
    feat = w_up.shape[0]
    per_owner = w_up.shape[1] // BLK
    anywhere = pl.BlockSpec(memory_space=pl.ANY)
    return pl.pallas_call(
        functools.partial(up_kernel, per_owner),
        in_specs=[pl.BlockSpec(memory_space=pltpu.SMEM)] + [anywhere] * (len(parts) + 1),
        out_specs=[anywhere] * 2,
        scratch_shapes=[
            pltpu.VMEM((PLANE, BLK, feat), jnp.bfloat16),
            pltpu.VMEM((DEPTH, feat, 2 * BLK), jnp.bfloat16),
            pltpu.VMEM((2, 2, BLK, BLK), jnp.float32),
            pltpu.VMEM((2, 2, BLK, BLK), jnp.bfloat16),
            pltpu.SemaphoreType.DMA((len(parts),)),
            pltpu.SemaphoreType.DMA((DEPTH, 2)),
            pltpu.SemaphoreType.DMA((2,)),
            pltpu.SemaphoreType.DMA((2,)),
        ],
        out_shape=[
            jax.ShapeDtypeStruct((slots, BLK, BLK), jnp.float32),
            jax.ShapeDtypeStruct((slots, BLK, BLK), jnp.bfloat16),
        ],
        compiler_params=pltpu.CompilerParams(vmem_limit_bytes=VMEM_BYTES),
        cost_estimate=estimate(feat),
        name="up_group",
    )(meta, *parts, w_up)


def down_kernel(per_owner, slots, meta, own_ref, other_ref, bias_ref, w_ref, *refs):
    outs, (total, held, own, other, done, sems, done_sems) = refs[:PLANE + 1], refs[PLANE + 1:]
    count = meta[0]
    width = total.shape[1]
    piece = width // 6 if width % (6 * BLK) == 0 else width

    def results(o):
        if o < PLANE - 1:
            return [pltpu.make_async_copy(done.at[o], outs[o], done_sems.at[o])]
        halves = [pl.ds(0, HALF), pl.ds(HALF, HALF)]
        return [pltpu.make_async_copy(done.at[o, half], outs[o + at], done_sems.at[o + at]) for at, half in enumerate(halves)]

    def copies_of(step, slot):
        pair = pl.ds(2 * step, 2)
        yield pltpu.make_async_copy(own_ref.at[pair], own.at[slot], sems.at[slot, 2]), None
        yield pltpu.make_async_copy(other_ref.at[pair], other.at[slot], sems.at[slot, 3]), None
        left, right = meta[1 + 2 * step], meta[2 + 2 * step]
        for side, code in enumerate((left, jnp.where(right < 0, left, right))):
            rows = pl.ds(pl.multiple_of(lax.rem(code, per_owner) * BLK, BLK), BLK)
            place = held.at[slot, pl.ds(side * BLK, BLK)]
            yield pltpu.make_async_copy(w_ref.at[rows], place, sems.at[slot, side]), None

    def hidden_of(slot, side, code):
        preact = own[slot, side] + other[slot, side].astype(jnp.float32) + bias_ref[lax.rem(code, per_owner)]
        return jnp.maximum(preact, 0.0)

    def use(step, slot):
        left, right = meta[1 + 2 * step], meta[2 + 2 * step]
        offset = lax.div(left, per_owner)
        before = lax.div(meta[jnp.maximum(2 * step - 1, 1)], per_owner)
        after = lax.div(meta[3 + 2 * step], per_owner)
        first = (step == 0) | (before != offset)
        last = (step >= count - 1) | (after != offset)
        one = hidden_of(slot, 0, left)
        two = jnp.where(right < 0, 0.0, hidden_of(slot, 1, jnp.maximum(right, 0)))
        hidden = jnp.concatenate([one, two], axis=1).astype(jnp.bfloat16)
        for is_first in (True, False):
            for is_last in (True, False):
                @pl.when((first == is_first) & (last == is_last))
                def _():
                    for at in range(0, width, piece):
                        cols = pl.ds(at, piece)
                        term = jnp.dot(hidden, held[slot, :, cols], preferred_element_type=jnp.float32)
                        if not is_first:
                            term = total[:, cols] + term
                        if is_last:
                            done[offset, :, cols] = term.astype(jnp.bfloat16)
                        else:
                            total[:, cols] = term

        for o in range(PLANE):
            @pl.when(last & (offset == o))
            def _():
                for copy in results(o):
                    copy.start()

    stream(meta, count, copies_of, lambda: None, use)
    for o in range(PLANE):
        @pl.when(meta[1 + slots + 2 + o] == 0)
        def _():
            done[o] = jnp.zeros_like(done[o])
            for copy in results(o):
                copy.start()

    for o in range(PLANE):
        for copy in results(o):
            copy.wait()


def down_group(meta, own, other, bias, w_down):
    feat = w_down.shape[1]
    per_owner = w_down.shape[0] // BLK
    anywhere = pl.BlockSpec(memory_space=pl.ANY)
    whole = pl.BlockSpec(memory_space=pltpu.VMEM)
    return pl.pallas_call(
        functools.partial(down_kernel, per_owner, own.shape[0]),
        in_specs=[pl.BlockSpec(memory_space=pltpu.SMEM), anywhere, anywhere, whole, anywhere],
        out_specs=[anywhere] * (PLANE + 1),
        scratch_shapes=[
            pltpu.VMEM((BLK, feat), jnp.float32),
            pltpu.VMEM((DEPTH, 2 * BLK, feat), jnp.bfloat16),
            pltpu.VMEM((DEPTH, 2, BLK, BLK), jnp.float32),
            pltpu.VMEM((DEPTH, 2, BLK, BLK), jnp.bfloat16),
            pltpu.VMEM((PLANE, BLK, feat), jnp.bfloat16),
            pltpu.SemaphoreType.DMA((DEPTH, 4)),
            pltpu.SemaphoreType.DMA((PLANE + 1,)),
        ],
        out_shape=[jax.ShapeDtypeStruct((rows, feat), jnp.bfloat16) for rows in (BLK, BLK, BLK, HALF, HALF)],
        compiler_params=pltpu.CompilerParams(vmem_limit_bytes=VMEM_BYTES),
        cost_estimate=estimate(feat),
        name="down_group",
    )(meta, own, other, bias, w_down)


def add_kernel(x_ref, y_ref, x_add, y_add, x_out, y_out):
    x_out[...] = (x_ref[...].astype(jnp.float32) + x_add[...].astype(jnp.float32)).astype(jnp.bfloat16)
    y_out[...] = (y_ref[...].astype(jnp.float32) + y_add[...].astype(jnp.float32)).astype(jnp.bfloat16)


def add_diagonal(over_x, over_y, x_add, y_add):
    feat = over_x.shape[1]
    steps = 6 if feat % (6 * BLK) == 0 else 1
    upper = pl.BlockSpec((HALF, feat // steps), lambda i: (0, i))
    lower = pl.BlockSpec((HALF, feat // steps), lambda i: (1, i))
    return pl.pallas_call(
        add_kernel,
        grid=(steps,),
        in_specs=[upper, lower, upper, upper],
        out_specs=[upper, lower],
        out_shape=[jax.ShapeDtypeStruct(over_x.shape, jnp.bfloat16)] * 2,
        input_output_aliases={0: 0, 1: 1},
        name="add_diagonal",
    )(over_x, over_y, x_add, y_add)


def swap(value, bits):
    return lax.ppermute(value, "wa", [(w, w ^ bits) for w in range(LAYERS * PLANE)])


def add(*terms):
    total = terms[0].astype(jnp.float32)
    for term in terms[1:]:
        total = total + term.astype(jnp.float32)
    return total


def narrow(*terms):
    return add(*terms).astype(jnp.bfloat16)


def pair_lists(active, owner, per_owner):
    layer, cell = owner // PLANE, owner % PLANE
    order = jnp.array([[0, 1, 2, 3], [1, 0, 2, 3], [2, 3, 1, 0], [3, 2, 1, 0]], jnp.int32)
    layers = jnp.sum(jnp.where(jnp.arange(LAYERS)[:, None] == layer, order, 0), axis=0)
    blocks = layers[:, None] * PLANE + (cell ^ jnp.arange(PLANE, dtype=jnp.int32))[None, :]
    targets = owner * per_owner + jnp.arange(per_owner, dtype=jnp.int32)
    hits = jnp.any(active[:, :, None] == targets[None, None, :], axis=1)
    is_block = blocks[:, :, None] == jnp.arange(active.shape[0], dtype=jnp.int32)
    hits = jnp.any(is_block[..., None] & hits[None, None], axis=2).astype(jnp.int32)
    counts = jnp.sum(hits, axis=2)
    padded = counts + counts % 2
    starts = jnp.cumsum(padded, axis=1) - padded
    number = (starts[:, :, None] + jnp.cumsum(hits, axis=2)) * hits
    number = number.reshape(LAYERS, PLANE * per_owner)
    slots = 2 * per_owner + PLANE
    codes = jnp.arange(PLANE * per_owner, dtype=jnp.int32) + 1
    wanted = jnp.arange(slots, dtype=jnp.int32) + 1
    lists = jnp.sum(jnp.where(number[:, :, None] == wanted, codes[None, :, None], 0), axis=1) - 1
    steps = jnp.sum(padded, axis=1, keepdims=True) // 2
    return jnp.concatenate([steps, lists, jnp.full((LAYERS, 2), -1, jnp.int32), counts], axis=1), slots


def along_z(value, *hops):
    pairs = [(a * PLANE + q, b * PLANE + q) for a, b in hops for q in range(PLANE)]
    return lax.ppermute(value, "wa", pairs)


def together(*values):
    return lax.optimization_barrier(values)


def sides(block):
    return swap(block, 1), swap(block, 2)


def sides2(blocks):
    return swap(blocks[0], 1), swap(blocks[1], 2)


def corner(over_x, over_y):
    return swap(over_x[:HALF], 2), swap(over_y[HALF:], 1)


def by_layers(tokens, active, w_up, b_up, w_down, b_down):
    per_owner = w_up.shape[1] // BLK
    owner = lax.axis_index("wa")
    inner = (owner // PLANE == 1) | (owner // PLANE == 2)
    meta, slots = pair_lists(active, owner, per_owner)
    bias = b_up.reshape(per_owner, 1, BLK)

    def up(at, block, side, diagonal):
        return up_group(meta[at], [block, *side, *diagonal], w_up, slots)

    def down(at, sums):
        other = lax.ppermute(sums[1], "row", [(0, 1), (1, 0)])
        return down_group(meta[at], sums[0], other, bias, w_down)

    def cross(partial):
        return swap(partial[3], 2), swap(partial[4], 1)

    def summed(partial, crossed):
        return add_diagonal(partial[1], partial[2], *crossed)

    near, middle, side0 = swap(tokens, PLANE), along_z(tokens, (1, 2), (2, 1)), sides(tokens)
    near, middle, side0 = together(near, middle, side0)
    diag0, side1 = corner(*side0), sides(near)
    across, outward = along_z(near, (1, 2), (2, 1)), along_z(middle, (1, 0), (2, 3))
    across, outward, side1, diag0 = together(across, outward, side1, diag0)
    far = jnp.where(inner, middle, outward)
    diag1, side2, outward = corner(*side1), sides(far), along_z(across, (1, 0), (2, 3))
    up0 = up(0, tokens, side0, diag0)
    outward, side2, diag1, up0 = together(outward, side2, diag1, up0)
    last = jnp.where(inner, across, outward)
    diag2, side3 = corner(*side2), sides(last)
    part0, up1 = down(0, up0), up(1, near, side1, diag1)
    side3, diag2, part0, up1 = together(side3, diag2, part0, up1)
    diag3, cross0 = corner(*side3), cross(part0)
    part1, up2 = down(1, up1), up(2, far, side2, diag2)
    up3 = up(3, last, side3, diag3)
    cross0, part1, up2, up3 = together(cross0, part1, up2, up3)
    cross1, part2, part3 = cross(part1), down(2, up2), down(3, up3)
    cross1, part2, part3 = together(cross1, part2, part3)
    cross3, cross2 = cross(part3), cross(part2)
    sent3 = summed(part3, cross3)
    sent3, cross2, part1, cross1, part0, cross0 = together(sent3, cross2, part1, cross1, part0, cross0)
    got3 = sides2(sent3)
    sent2 = summed(part2, cross2)
    got2 = sides2(sent2)
    sum3 = narrow(part3[0], *got3)
    passed = along_z(sum3, (0, 1), (3, 2))
    sent1, sent0 = summed(part1, cross1), summed(part0, cross0)
    got2, sum3, sent1, sent0 = together(got2, sum3, sent1, sent0)
    got1, got0 = sides2(sent1), sides2(sent0)
    sum2 = narrow(part2[0], *got2)
    passed = along_z(narrow(sum3, passed), (1, 2), (2, 1))
    inward = along_z(sum2, (0, 1), (3, 2))
    near = swap(narrow(part1[0], passed, *got1), PLANE)
    middle = along_z(narrow(sum2, inward), (1, 2), (2, 1))
    return (add(part0[0], *got0, near, middle) + b_down).astype(jnp.bfloat16)


def general(tokens, active, w_up, b_up, w_down, b_down):
    feat_dev = tokens.shape[1]
    tblocks = active.shape[0]
    owners = lax.axis_size("wa")
    per_owner = w_up.shape[1] // BLK
    nblocks = per_owner * owners
    capacity = max(2, 5 * tblocks * K // (4 * nblocks))
    gathered = lax.all_gather(tokens, "wa", axis=0, tiled=True)
    token_blocks = gathered.reshape(tblocks, BLK, feat_dev)
    owner = lax.axis_index("wa")
    targets = owner * per_owner + jnp.arange(per_owner, dtype=jnp.int32)
    hits = jnp.any(active[:, :, None] == targets[None, None, :], axis=1).astype(jnp.int32)
    running = jnp.cumsum(hits, axis=0)
    slots = jnp.arange(capacity, dtype=jnp.int32) + 1
    picked = hits[:, :, None] * (running[:, :, None] == slots[None, None, :]).astype(jnp.int32)
    block_index = jnp.arange(tblocks, dtype=jnp.int32)
    slot_tok = jnp.sum(picked * block_index[:, None, None], axis=0)
    selected = token_blocks[slot_tok.reshape(-1)].reshape(per_owner, capacity * BLK, feat_dev)
    up_local = w_up.reshape(feat_dev, per_owner, BLK)
    preact = jnp.einsum("jmd,djb->jmb", selected, up_local, preferred_element_type=jnp.float32)
    bias_local = b_up.reshape(per_owner, 1, BLK)
    summed = lax.psum(preact.astype(jnp.bfloat16), "row").astype(jnp.float32)
    hidden = jnp.maximum(summed + bias_local, 0.0).astype(jnp.bfloat16)
    down_local = w_down.reshape(per_owner, BLK, feat_dev)
    contrib = jnp.einsum("jmb,jbd->jmd", hidden, down_local, preferred_element_type=jnp.float32)
    contrib = contrib.reshape(per_owner, capacity, BLK, feat_dev)
    placing = picked.transpose(1, 2, 0).astype(jnp.float32)
    partial_value = jnp.einsum("jct,jcqd->tqd", placing, contrib, precision=lax.Precision.HIGHEST)
    terms = partial_value.reshape(tblocks * BLK, feat_dev).astype(jnp.bfloat16)
    total = lax.psum_scatter(terms, "wa", scatter_dimension=0, tiled=True).astype(jnp.float32)
    return (total + b_down).astype(jnp.bfloat16)


def solution(mesh):
    sizes = (mesh.shape["wa"], mesh.shape["row"])
    per_device = by_layers if sizes == (LAYERS * PLANE, 2) else general
    in_specs = (P("wa", "row"), P(), P("row", "wa"), P("wa"), P("wa", "row"), P("row"))
    out_specs = P("wa", "row")
    return jax.shard_map(
        per_device, mesh=mesh, in_specs=in_specs, out_specs=out_specs, check_vma=False
    )
```

```python
import functools

import jax
import jax.numpy as jnp
from jax import lax
from jax.experimental import pallas as pl
from jax.experimental.pallas import tpu as pltpu
from jax.sharding import PartitionSpec as P

BLK = 128
K = 48
HALF = BLK // 2
PLANE = 4
LAYERS = 4
DEPTH = 5
VMEM_BYTES = 56 * 1024 * 1024


def stream(meta, count, copies_of, ready, use):
    def each(step, slot, act):
        for copy, wanted in copies_of(step, slot):
            if wanted is None:
                act(copy)
            else:
                pl.when(wanted)(functools.partial(act, copy))

    def start(step, slot):
        each(step, slot, lambda copy: copy.start())

    for ahead in range(DEPTH - 1):
        @pl.when(ahead < count)
        def _():
            start(ahead, ahead)

    ready()

    def body(step, carry):
        nearest = step + DEPTH - 1

        @pl.when(nearest < count)
        def _():
            start(nearest, lax.rem(nearest, DEPTH))

        slot = lax.rem(step, DEPTH)
        each(step, slot, lambda copy: copy.wait())
        use(step, slot)
        return carry

    lax.fori_loop(0, count, body, 0)


def up_kernel(per_owner, meta, *refs):
    count_of = len(refs) - 11
    parts, refs = refs[:count_of], refs[count_of:]
    w_ref, own_ref, send_ref, rows, held, own, send, row_sems, sems, own_sems, send_sems = refs
    count = meta[0]
    places, first = [], 0
    for part in parts:
        places.append(rows.at[first // BLK, pl.ds(first % BLK, part.shape[0])])
        first += part.shape[0]
    copies = [pltpu.make_async_copy(*ends, row_sems.at[at]) for at, ends in enumerate(zip(parts, places))]
    for copy in copies:
        copy.start()

    def ready():
        for copy in copies:
            copy.wait()

    def copies_of(step, slot):
        for side in range(2):
            code = meta[1 + 2 * step + side]
            block = lax.rem(jnp.maximum(code, 0), per_owner)
            cols = pl.ds(pl.multiple_of(block * BLK, BLK), BLK)
            place = held.at[slot, :, pl.ds(side * BLK, BLK)]
            yield pltpu.make_async_copy(w_ref.at[:, cols], place, sems.at[slot, side]), code >= 0 if side else None

    def results(step):
        slot = lax.rem(step, 2)
        pair = pl.ds(2 * step, 2)
        return (pltpu.make_async_copy(own.at[slot], own_ref.at[pair], own_sems.at[slot]),
                pltpu.make_async_copy(send.at[slot], send_ref.at[pair], send_sems.at[slot]))

    def use(step, slot):
        offset = lax.div(meta[1 + 2 * step], per_owner)
        preact = jnp.dot(rows[offset], held[slot], preferred_element_type=jnp.float32)

        @pl.when(step >= 2)
        def _():
            for copy in results(step - 2):
                copy.wait()

        at = lax.rem(step, 2)
        for side in range(2):
            cols = slice(side * BLK, (side + 1) * BLK)
            own[at, side] = preact[:, cols]
            send[at, side] = preact[:, cols].astype(jnp.bfloat16)
        for copy in results(step):
            copy.start()

    stream(meta, count, copies_of, ready, use)
    for back in (2, 1):
        @pl.when(count >= back)
        def _():
            for copy in results(count - back):
                copy.wait()


def estimate(feat):
    return pl.CostEstimate(flops=2 * BLK * BLK * feat, bytes_accessed=BLK * feat * 2, transcendentals=0)


def up_group(meta, parts, w_up, slots):
    feat = w_up.shape[0]
    per_owner = w_up.shape[1] // BLK
    anywhere = pl.BlockSpec(memory_space=pl.ANY)
    return pl.pallas_call(
        functools.partial(up_kernel, per_owner),
        in_specs=[pl.BlockSpec(memory_space=pltpu.SMEM)] + [anywhere] * (len(parts) + 1),
        out_specs=[anywhere] * 2,
        scratch_shapes=[
            pltpu.VMEM((PLANE, BLK, feat), jnp.bfloat16),
            pltpu.VMEM((DEPTH, feat, 2 * BLK), jnp.bfloat16),
            pltpu.VMEM((2, 2, BLK, BLK), jnp.float32),
            pltpu.VMEM((2, 2, BLK, BLK), jnp.bfloat16),
            pltpu.SemaphoreType.DMA((len(parts),)),
            pltpu.SemaphoreType.DMA((DEPTH, 2)),
            pltpu.SemaphoreType.DMA((2,)),
            pltpu.SemaphoreType.DMA((2,)),
        ],
        out_shape=[
            jax.ShapeDtypeStruct((slots, BLK, BLK), jnp.float32),
            jax.ShapeDtypeStruct((slots, BLK, BLK), jnp.bfloat16),
        ],
        compiler_params=pltpu.CompilerParams(vmem_limit_bytes=VMEM_BYTES),
        cost_estimate=estimate(feat),
        name="up_group",
    )(meta, *parts, w_up)


def down_kernel(per_owner, slots, meta, own_ref, other_ref, bias_ref, w_ref, *refs):
    outs, (total, held, own, other, done, sems, done_sems) = refs[:PLANE + 1], refs[PLANE + 1:]
    count = meta[0]
    width = total.shape[1]
    piece = width // 6 if width % (6 * BLK) == 0 else width

    def results(o):
        if o < PLANE - 1:
            return [pltpu.make_async_copy(done.at[o], outs[o], done_sems.at[o])]
        halves = [pl.ds(0, HALF), pl.ds(HALF, HALF)]
        return [pltpu.make_async_copy(done.at[o, half], outs[o + at], done_sems.at[o + at]) for at, half in enumerate(halves)]

    def copies_of(step, slot):
        pair = pl.ds(2 * step, 2)
        yield pltpu.make_async_copy(own_ref.at[pair], own.at[slot], sems.at[slot, 2]), None
        yield pltpu.make_async_copy(other_ref.at[pair], other.at[slot], sems.at[slot, 3]), None
        left, right = meta[1 + 2 * step], meta[2 + 2 * step]
        for side, code in enumerate((left, jnp.where(right < 0, left, right))):
            rows = pl.ds(pl.multiple_of(lax.rem(code, per_owner) * BLK, BLK), BLK)
            place = held.at[slot, pl.ds(side * BLK, BLK)]
            yield pltpu.make_async_copy(w_ref.at[rows], place, sems.at[slot, side]), None

    def hidden_of(slot, side, code):
        preact = own[slot, side] + other[slot, side].astype(jnp.float32) + bias_ref[lax.rem(code, per_owner)]
        return jnp.maximum(preact, 0.0)

    def use(step, slot):
        left, right = meta[1 + 2 * step], meta[2 + 2 * step]
        offset = lax.div(left, per_owner)
        before = lax.div(meta[jnp.maximum(2 * step - 1, 1)], per_owner)
        after = lax.div(meta[3 + 2 * step], per_owner)
        first = (step == 0) | (before != offset)
        last = (step >= count - 1) | (after != offset)
        one = hidden_of(slot, 0, left)
        two = jnp.where(right < 0, 0.0, hidden_of(slot, 1, jnp.maximum(right, 0)))
        hidden = jnp.concatenate([one, two], axis=1).astype(jnp.bfloat16)
        for is_first in (True, False):
            for is_last in (True, False):
                @pl.when((first == is_first) & (last == is_last))
                def _():
                    for at in range(0, width, piece):
                        cols = pl.ds(at, piece)
                        term = jnp.dot(hidden, held[slot, :, cols], preferred_element_type=jnp.float32)
                        if not is_first:
                            term = total[:, cols] + term
                        if is_last:
                            done[offset, :, cols] = term.astype(jnp.bfloat16)
                        else:
                            total[:, cols] = term

        for o in range(PLANE):
            @pl.when(last & (offset == o))
            def _():
                for copy in results(o):
                    copy.start()

    stream(meta, count, copies_of, lambda: None, use)
    for o in range(PLANE):
        @pl.when(meta[1 + slots + 2 + o] == 0)
        def _():
            done[o] = jnp.zeros_like(done[o])
            for copy in results(o):
                copy.start()

    for o in range(PLANE):
        for copy in results(o):
            copy.wait()


def down_group(meta, own, other, bias, w_down):
    feat = w_down.shape[1]
    per_owner = w_down.shape[0] // BLK
    anywhere = pl.BlockSpec(memory_space=pl.ANY)
    whole = pl.BlockSpec(memory_space=pltpu.VMEM)
    return pl.pallas_call(
        functools.partial(down_kernel, per_owner, own.shape[0]),
        in_specs=[pl.BlockSpec(memory_space=pltpu.SMEM), anywhere, anywhere, whole, anywhere],
        out_specs=[anywhere] * (PLANE + 1),
        scratch_shapes=[
            pltpu.VMEM((BLK, feat), jnp.float32),
            pltpu.VMEM((DEPTH, 2 * BLK, feat), jnp.bfloat16),
            pltpu.VMEM((DEPTH, 2, BLK, BLK), jnp.float32),
            pltpu.VMEM((DEPTH, 2, BLK, BLK), jnp.bfloat16),
            pltpu.VMEM((PLANE, BLK, feat), jnp.bfloat16),
            pltpu.SemaphoreType.DMA((DEPTH, 4)),
            pltpu.SemaphoreType.DMA((PLANE + 1,)),
        ],
        out_shape=[jax.ShapeDtypeStruct((rows, feat), jnp.bfloat16) for rows in (BLK, BLK, BLK, HALF, HALF)],
        compiler_params=pltpu.CompilerParams(vmem_limit_bytes=VMEM_BYTES),
        cost_estimate=estimate(feat),
        name="down_group",
    )(meta, own, other, bias, w_down)


def add_kernel(x_ref, y_ref, x_add, y_add, x_out, y_out):
    x_out[...] = (x_ref[...].astype(jnp.float32) + x_add[...].astype(jnp.float32)).astype(jnp.bfloat16)
    y_out[...] = (y_ref[...].astype(jnp.float32) + y_add[...].astype(jnp.float32)).astype(jnp.bfloat16)


def add_diagonal(over_x, over_y, x_add, y_add):
    feat = over_x.shape[1]
    steps = 3
    upper = pl.BlockSpec((HALF, feat // steps), lambda i: (0, i))
    lower = pl.BlockSpec((HALF, feat // steps), lambda i: (1, i))
    return pl.pallas_call(
        add_kernel,
        grid=(steps,),
        in_specs=[upper, lower, upper, upper],
        out_specs=[upper, lower],
        out_shape=[jax.ShapeDtypeStruct(over_x.shape, jnp.bfloat16)] * 2,
        input_output_aliases={0: 0, 1: 1},
        name="add_diagonal",
    )(over_x, over_y, x_add, y_add)


def swap(value, bits):
    return lax.ppermute(value, "wa", [(w, w ^ bits) for w in range(LAYERS * PLANE)])


def add(*terms):
    total = terms[0].astype(jnp.float32)
    for term in terms[1:]:
        total = total + term.astype(jnp.float32)
    return total


def narrow(*terms):
    return add(*terms).astype(jnp.bfloat16)


def pair_lists(active, owner, per_owner):
    layer, cell = owner // PLANE, owner % PLANE
    order = jnp.array([[0, 1, 2, 3], [1, 0, 2, 3], [2, 3, 1, 0], [3, 2, 1, 0]], jnp.int32)
    layers = jnp.sum(jnp.where(jnp.arange(LAYERS)[:, None] == layer, order, 0), axis=0)
    blocks = layers[:, None] * PLANE + (cell ^ jnp.arange(PLANE, dtype=jnp.int32))[None, :]
    targets = owner * per_owner + jnp.arange(per_owner, dtype=jnp.int32)
    hits = jnp.any(active[:, :, None] == targets[None, None, :], axis=1)
    is_block = blocks[:, :, None] == jnp.arange(active.shape[0], dtype=jnp.int32)
    hits = jnp.any(is_block[..., None] & hits[None, None], axis=2).astype(jnp.int32)
    counts = jnp.sum(hits, axis=2)
    padded = counts + counts % 2
    starts = jnp.cumsum(padded, axis=1) - padded
    number = (starts[:, :, None] + jnp.cumsum(hits, axis=2)) * hits
    number = number.reshape(LAYERS, PLANE * per_owner)
    slots = 2 * per_owner + PLANE
    codes = jnp.arange(PLANE * per_owner, dtype=jnp.int32) + 1
    wanted = jnp.arange(slots, dtype=jnp.int32) + 1
    lists = jnp.sum(jnp.where(number[:, :, None] == wanted, codes[None, :, None], 0), axis=1) - 1
    steps = jnp.sum(padded, axis=1, keepdims=True) // 2
    return jnp.concatenate([steps, lists, jnp.full((LAYERS, 2), -1, jnp.int32), counts], axis=1), slots


def along_z(value, *hops):
    pairs = [(a * PLANE + q, b * PLANE + q) for a, b in hops for q in range(PLANE)]
    return lax.ppermute(value, "wa", pairs)


def together(*values):
    return lax.optimization_barrier(values)


def sides(block):
    return swap(block, 1), swap(block, 2)


def sides2(blocks):
    return swap(blocks[0], 1), swap(blocks[1], 2)


def corner(over_x, over_y):
    return swap(over_x[:HALF], 2), swap(over_y[HALF:], 1)


def by_layers(tokens, active, w_up, b_up, w_down, b_down):
    per_owner = w_up.shape[1] // BLK
    owner = lax.axis_index("wa")
    inner = (owner // PLANE == 1) | (owner // PLANE == 2)
    meta, slots = pair_lists(active, owner, per_owner)
    bias = b_up.reshape(per_owner, 1, BLK)

    def up(at, block, side, diagonal):
        return up_group(meta[at], [block, *side, *diagonal], w_up, slots)

    def down(at, sums):
        other = lax.ppermute(sums[1], "row", [(0, 1), (1, 0)])
        return down_group(meta[at], sums[0], other, bias, w_down)

    def cross(partial):
        return swap(partial[3], 2), swap(partial[4], 1)

    def summed(partial, crossed):
        return add_diagonal(partial[1], partial[2], *crossed)

    near, middle, side0 = swap(tokens, PLANE), along_z(tokens, (1, 2), (2, 1)), sides(tokens)
    near, middle, side0 = together(near, middle, side0)
    diag0, side1 = corner(*side0), sides(near)
    across, outward = along_z(near, (1, 2), (2, 1)), along_z(middle, (1, 0), (2, 3))
    across, outward, side1, diag0 = together(across, outward, side1, diag0)
    far = jnp.where(inner, middle, outward)
    diag1, side2, outward = corner(*side1), sides(far), along_z(across, (1, 0), (2, 3))
    up0 = up(0, tokens, side0, diag0)
    outward, side2, diag1, up0 = together(outward, side2, diag1, up0)
    last = jnp.where(inner, across, outward)
    diag2 = corner(*side2)
    side3 = [swap(last[rows], bit) for bit in (1, 2) for rows in (slice(0, HALF), slice(HALF, BLK))]
    part0, up1, up2 = down(0, up0), up(1, near, side1, diag1), up(2, far, side2, diag2)
    side3, part0, up1, up2 = together(side3, part0, up1, up2)
    diag3, cross0 = (swap(side3[0], 2), swap(side3[3], 1)), cross(part0)
    part1 = down(1, up1)
    diag3, part1 = together(diag3, part1)
    up3 = up(3, last, side3, diag3)
    cross0, part1, up2, up3 = together(cross0, part1, up2, up3)
    cross1, part2, part3 = cross(part1), down(2, up2), down(3, up3)
    cross1, part2, part3 = together(cross1, part2, part3)
    cross3, cross2 = cross(part3), cross(part2)
    sent3 = summed(part3, cross3)
    sent3, cross2, part1, cross1, part0, cross0 = together(sent3, cross2, part1, cross1, part0, cross0)
    got3 = sides2(sent3)
    sent2 = summed(part2, cross2)
    got2 = sides2(sent2)
    sum3 = narrow(part3[0], *got3)
    passed = along_z(sum3, (0, 1), (3, 2))
    sent1, sent0 = summed(part1, cross1), summed(part0, cross0)
    got2, sum3, sent1, sent0 = together(got2, sum3, sent1, sent0)
    got1, got0 = sides2(sent1), sides2(sent0)
    sum2 = narrow(part2[0], *got2)
    passed = along_z(narrow(sum3, passed), (1, 2), (2, 1))
    inward = along_z(sum2, (0, 1), (3, 2))
    near = swap(narrow(part1[0], passed, *got1), PLANE)
    middle = along_z(narrow(sum2, inward), (1, 2), (2, 1))
    return (add(part0[0], *got0, near, middle) + b_down).astype(jnp.bfloat16)


def general(tokens, active, w_up, b_up, w_down, b_down):
    feat_dev = tokens.shape[1]
    tblocks = active.shape[0]
    owners = lax.axis_size("wa")
    per_owner = w_up.shape[1] // BLK
    nblocks = per_owner * owners
    capacity = max(2, 5 * tblocks * K // (4 * nblocks))
    gathered = lax.all_gather(tokens, "wa", axis=0, tiled=True)
    token_blocks = gathered.reshape(tblocks, BLK, feat_dev)
    owner = lax.axis_index("wa")
    targets = owner * per_owner + jnp.arange(per_owner, dtype=jnp.int32)
    hits = jnp.any(active[:, :, None] == targets[None, None, :], axis=1).astype(jnp.int32)
    running = jnp.cumsum(hits, axis=0)
    slots = jnp.arange(capacity, dtype=jnp.int32) + 1
    picked = hits[:, :, None] * (running[:, :, None] == slots[None, None, :]).astype(jnp.int32)
    block_index = jnp.arange(tblocks, dtype=jnp.int32)
    slot_tok = jnp.sum(picked * block_index[:, None, None], axis=0)
    selected = token_blocks[slot_tok.reshape(-1)].reshape(per_owner, capacity * BLK, feat_dev)
    up_local = w_up.reshape(feat_dev, per_owner, BLK)
    preact = jnp.einsum("jmd,djb->jmb", selected, up_local, preferred_element_type=jnp.float32)
    bias_local = b_up.reshape(per_owner, 1, BLK)
    summed = lax.psum(preact.astype(jnp.bfloat16), "row").astype(jnp.float32)
    hidden = jnp.maximum(summed + bias_local, 0.0).astype(jnp.bfloat16)
    down_local = w_down.reshape(per_owner, BLK, feat_dev)
    contrib = jnp.einsum("jmb,jbd->jmd", hidden, down_local, preferred_element_type=jnp.float32)
    contrib = contrib.reshape(per_owner, capacity, BLK, feat_dev)
    placing = picked.transpose(1, 2, 0).astype(jnp.float32)
    partial_value = jnp.einsum("jct,jcqd->tqd", placing, contrib, precision=lax.Precision.HIGHEST)
    terms = partial_value.reshape(tblocks * BLK, feat_dev).astype(jnp.bfloat16)
    total = lax.psum_scatter(terms, "wa", scatter_dimension=0, tiled=True).astype(jnp.float32)
    return (total + b_down).astype(jnp.bfloat16)


def solution(mesh):
    sizes = (mesh.shape["wa"], mesh.shape["row"])
    per_device = by_layers if sizes == (LAYERS * PLANE, 2) else general
    in_specs = (P("wa", "row"), P(), P("row", "wa"), P("wa"), P("wa", "row"), P("row"))
    out_specs = P("wa", "row")
    return jax.shard_map(
        per_device, mesh=mesh, in_specs=in_specs, out_specs=out_specs, check_vma=False
    )
```
